32 devices in a mesh: rows: 16 (over z, x, core), chan: 2 (over y).
Axes of the slice: x: 2, y: 2, z: 4, core: 2. Of those that a mesh axis runs over, the one named last changes fastest.
Arguments:
- hidden: float32 [32, 512, 2048], P('chan', 'rows'), may hold values from -6 to 6
- front: float32 [512, 2048], P('rows', 'chan'), may hold values from -6 to 6
- spectral_weight: float32 [2, 128, 128, 32, 32], P(None, 'rows', 'chan'), may hold values from -0.5 to 0.5
- skip_gain: float32 [32], P('chan'), may hold values from 0.5 to 1.5
- skip_bias: float32 [32], P('chan'), may hold values from -3 to 3
- project_weight: float32 [2, 32], P(None, 'chan'), may hold values from -1 to 1
- project_bias: float32 [2], replicated, may hold values from -3 to 3
- ice_mask: int32 [512, 2048], P('rows', 'chan'), may hold values 0 or 1
- front_flags: int32 [512, 2048], P('rows', 'chan'), may hold values 0 or 1
Outputs:
- velocity: float32 [2, 512, 2048], P(None, 'rows', 'chan')
- front_next: float32 [512, 2048], P('rows', 'chan')
The draws below stay inside these ranges and needn't reach their ends.
All inputs are finite; a program needn't handle non-finite values. No bound on the sum of `ice_mask` or of `front_flags` on one device may be relied on, other than what follows from the above.
Results may differ from the reference program's by a relative error of at most 0.0003.
Values sent between devices are 32-bit elements; how exact they have to be, the bound alone decides.
A program may use at most 128 MiB of HBM per device.

```python
import math
import jax
import jax.numpy as jnp
from jax import lax

C = 32
MX = 128
MY = 128
NY = 2048
LS_STEPS = 4
NX = 512


def set_ends(result, rng, smallest, high):
    index_at = [jax.random.randint(jax.random.fold_in(rng, axis), (), 0, length) for axis, length in enumerate(result.shape)]
    main_axis = result.shape.index(max(result.shape))
    neighbour = index_at[:main_axis] + [(index_at[main_axis] + 1) % result.shape[main_axis]] + index_at[main_axis + 1:]
    return result.at[tuple(index_at)].set(smallest).at[tuple(neighbour)].set(high)


def block_levels(rng, dims, shards, low, top_value):
    level = 1.0
    for dim, parts in shards:
        heights = jax.random.uniform(jax.random.fold_in(jax.random.fold_in(rng, 6), dim), (parts,), jnp.float32, low / len(shards), top_value / len(shards))
        level = level * jnp.repeat(jnp.exp(heights), dims[dim] // parts).reshape((-1,) + (1,) * (len(dims) - 1 - dim))
    return level


def normal_values(stream_key, dims, spread, reach, split=(), held_as=jnp.bfloat16):
    level = block_levels(stream_key, dims, split, -0.22, 0.18) if split else 1.0
    entries = jax.random.normal(stream_key, dims, jnp.float32) * spread * level
    return jnp.minimum(jnp.maximum(entries, -reach), reach).astype(held_as)


def setup_inputs(seed: int = 0) -> dict:
    keys = jax.random.split(jax.random.key(seed), 10)
    hidden = normal_values(keys[0], (C, NX, NY), 1.0, 6.0, ((0, 2), (1, 16)), jnp.float32)
    front = normal_values(keys[1], (NX, NY), 1.0, 6.0, ((0, 16), (1, 2)), jnp.float32)
    spectral_weight = normal_values(keys[2], (2, MY, MX, C, C), (4 * C) ** -0.5, 0.5, ((1, 16), (2, 2)), jnp.float32)
    skip_gain = jnp.clip(1.0 + 0.1 * jax.random.normal(keys[3], (C,), jnp.float32), 0.5, 1.5)
    skip_bias = normal_values(keys[4], (C,), 0.5, 3.0, ((0, 2),), jnp.float32)
    project_weight = normal_values(keys[5], (2, C), C ** -0.5, 1.0, ((1, 2),), jnp.float32)
    project_bias = normal_values(keys[6], (2,), 0.5, 3.0, (), jnp.float32)
    ice_mask = set_ends((jax.random.randint(keys[7], (NX, NY), 0, 4) < 3).astype(jnp.int32), jax.random.fold_in(keys[7], 1), 0, 1)
    front_flags = set_ends((jax.random.randint(keys[8], (NX, NY), 0, 2) < 1).astype(jnp.int32), jax.random.fold_in(keys[8], 1), 0, 1)
    return {"hidden": hidden, "front": front, "spectral_weight": spectral_weight, "skip_gain": skip_gain, "skip_bias": skip_bias, "project_weight": project_weight, "project_bias": project_bias, "ice_mask": ice_mask, "front_flags": front_flags}


time_step = 0.25

def advance(padded, speed_x, speed_y, band):
    center = padded[1:-1, 1:-1]
    back_x = center - padded[:-2, 1:-1]
    ahead_x = padded[2:, 1:-1] - center
    back_y = center - padded[1:-1, :-2]
    ahead_y = padded[1:-1, 2:] - center
    transport = jnp.maximum(speed_x, 0.0) * back_x + jnp.minimum(speed_x, 0.0) * ahead_x
    transport = transport + jnp.maximum(speed_y, 0.0) * back_y + jnp.minimum(speed_y, 0.0) * ahead_y
    return center - time_step * band * transport

def reference(hidden, front, spectral_weight, skip_gain, skip_bias, project_weight, project_bias, ice_mask, front_flags):
    highest = lax.Precision.HIGHEST
    half_modes = MX // 2
    spec_y = jnp.fft.rfft(hidden, axis=2)[:, :, :MY]
    spec_full = jnp.fft.fft(spec_y, axis=1)
    kept = jnp.concatenate([spec_full[:, :half_modes], spec_full[:, NX - half_modes:]], axis=1)
    complex_weight = spectral_weight[0] + 1j * spectral_weight[1]
    mixed = jnp.einsum('qpio,ipq->opq', complex_weight, kept, precision=highest)
    placed = jnp.zeros((C, NX, MY), mixed.dtype)
    placed = placed.at[:, :half_modes].set(mixed[:, :half_modes])
    placed = placed.at[:, NX - half_modes:].set(mixed[:, half_modes:])
    spectral = jnp.fft.irfft(jnp.fft.ifft(placed, axis=1), n=NY, axis=2)
    spectral = spectral * math.sqrt(NX * NY / (MX * MY))
    activated = jax.nn.gelu(spectral + skip_gain[:, None, None] * hidden + skip_bias[:, None, None], approximate=False)
    velocity = jnp.einsum('jc,cxy->jxy', project_weight, activated, precision=highest) + project_bias[:, None, None]
    velocity = velocity * ice_mask.astype(jnp.float32)[None]
    band = front_flags.astype(jnp.float32)
    level = front
    for level_step in range(LS_STEPS):
        level = advance(jnp.pad(level, 1), velocity[0], velocity[1], band)
    return (velocity, level)
```

```python
import math

import jax
import jax.numpy as jnp
import numpy as np
from jax import lax
from jax.sharding import PartitionSpec as P

LS_STEPS = 4
time_step = 0.25
high = lax.Precision.HIGH


def np_angles(freqs, places, length):
    return 2.0 * math.pi / length * ((freqs[:, None] * places[None, :]) % length)


def with_halo(block, axis, dim, width):
    count = lax.axis_size(axis)
    forward = [(i, i + 1) for i in range(count - 1)]
    backward = [(target, source) for source, target in forward]
    size = block.shape[dim]
    low = lax.ppermute(lax.slice_in_dim(block, size - width, None, axis=dim), axis, forward)
    up = lax.ppermute(lax.slice_in_dim(block, 0, width, axis=dim), axis, backward)
    return jnp.concatenate([low, block, up], axis=dim)


def advance(phi, u, v, band):
    center = phi[1:-1, 1:-1]
    back_x = center - phi[:-2, 1:-1]
    ahead_x = phi[2:, 1:-1] - center
    back_y = center - phi[1:-1, :-2]
    ahead_y = phi[1:-1, 2:] - center
    transport = jnp.maximum(u, 0.0) * back_x + jnp.minimum(u, 0.0) * ahead_x
    transport = transport + jnp.maximum(v, 0.0) * back_y + jnp.minimum(v, 0.0) * ahead_y
    return center - time_step * band * transport


def on_device(
    hidden,
    front,
    spectral_weight,
    skip_gain,
    skip_bias,
    project_weight,
    project_bias,
    ice_mask,
    front_flags,
):
    cl, rc, ny = hidden.shape
    R = lax.axis_size("rows")
    D = lax.axis_size("chan")
    ql = spectral_weight.shape[1]
    pl_ = spectral_weight.shape[2]
    nx = rc * R
    mx = pl_ * D
    my = ql * R
    scale = 1.0 / math.sqrt(nx * ny * mx * my)
    yph = np_angles(np.arange(my), np.arange(ny), ny)
    fy = np.stack([np.cos(yph), -np.sin(yph)], axis=1).reshape(2 * my, ny).astype(np.float32)
    w = np.where(np.arange(my) == 0, 1.0, 2.0)[:, None] * scale
    iy = np.stack([w * np.cos(yph), -w * np.sin(yph)], axis=1).reshape(2 * my, ny).astype(np.float32)
    pid = np.arange(mx)
    kp = np.where(pid < mx // 2, pid, pid - mx)
    xph = np_angles(kp, np.arange(nx), nx)
    cx = np.cos(xph).astype(np.float32)
    sx = np.sin(xph).astype(np.float32)
    fx = np.stack([np.stack([cx, -sx]), np.stack([sx, cx])]).transpose(0, 3, 1, 2).reshape(2, nx, 2 * mx)
    ix = np.stack([np.stack([cx, sx]), np.stack([-sx, cx])]).reshape(2, 2, mx, nx)

    spec_y = jnp.einsum("ky,cxy->kcx", jnp.asarray(fy), hidden, precision=high)
    recv = lax.all_to_all(spec_y.reshape(R, ql, 2, cl, rc), "rows", 0, 0, tiled=True)
    spec = jnp.einsum(
        "sqrcx,rsxP->qcP", recv, jnp.asarray(fx).reshape(2, R, rc, 2 * mx), precision=high
    ).reshape(ql, cl, 2, D, pl_)
    spec = lax.all_to_all(spec.transpose(3, 1, 2, 0, 4), "chan", 0, 0, tiled=True)
    spec = spec.reshape(D * cl, 2, ql, pl_)
    wt = spectral_weight.transpose(0, 3, 4, 1, 2)
    a, b = spec[:, 0][:, None], spec[:, 1][:, None]
    re = jnp.sum(wt[0] * a - wt[1] * b, axis=0)
    im = jnp.sum(wt[0] * b + wt[1] * a, axis=0)
    mixed = jnp.stack([re, im], axis=1).reshape(D, cl, 2, ql, pl_)
    mixed = lax.all_to_all(mixed, "chan", 0, 0, tiled=True)
    inv = jnp.einsum(
        "dcrqp,rtdpx->xqtc", mixed, jnp.asarray(ix).reshape(2, 2, D, pl_, nx), precision=high
    ).transpose(1, 2, 3, 0).reshape(ql, 2, cl, R, rc)
    inv = lax.all_to_all(inv.transpose(3, 0, 1, 2, 4), "rows", 0, 0, tiled=True)
    inv = inv.reshape(2 * my, cl, rc)
    spectral = jnp.einsum("kcx,ky->cxy", inv, jnp.asarray(iy), precision=high)
    act = jax.nn.gelu(
        spectral + skip_gain[:, None, None] * hidden + skip_bias[:, None, None], approximate=False
    )
    part = jnp.stack(
        [jnp.sum(project_weight[j][:, None, None] * act, axis=0) for j in range(2)]
    )
    part = part.reshape(2, rc, D, ny // D).transpose(2, 0, 1, 3)
    got = lax.all_to_all(part, "chan", 0, 0, tiled=True)
    speed = jnp.sum(got, axis=0) + project_bias[:, None, None]
    velocity = speed * ice_mask.astype(jnp.float32)[None]
    band = front_flags.astype(jnp.float32)
    W = LS_STEPS
    state = jnp.concatenate([velocity, band[None], front[None]], axis=0)
    state = with_halo(with_halo(state, "rows", 1, W), "chan", 2, W)
    u, v, bd, level = state[0], state[1], state[2], state[3]
    for step in range(LS_STEPS):
        i = step + 1
        level = advance(level, u[i:-i, i:-i], v[i:-i, i:-i], bd[i:-i, i:-i])
    return (velocity, level)


def solution(mesh):
    return jax.shard_map(
        on_device,
        mesh=mesh,
        in_specs=(
            P("chan", "rows", None),
            P("rows", "chan"),
            P(None, "rows", "chan", None, None),
            P("chan"),
            P("chan"),
            P(None, "chan"),
            P(),
            P("rows", "chan"),
            P("rows", "chan"),
        ),
        out_specs=(P(None, "rows", "chan"), P("rows", "chan")),
        check_vma=False,
    )
```

```python
import math

import jax
import jax.numpy as jnp
import numpy as np
from jax import lax
from jax.experimental import pallas as pl
from jax.experimental.pallas import tpu as pltpu
from jax.sharding import PartitionSpec as P

LS_STEPS = 4
time_step = 0.25
high = lax.Precision.HIGH


def np_angles(freqs, places, length):
    return 2.0 * math.pi / length * ((freqs[:, None] * places[None, :]) % length)


def with_halo(block, axis, dim, width):
    count = lax.axis_size(axis)
    forward = [(i, i + 1) for i in range(count - 1)]
    backward = [(target, source) for source, target in forward]
    size = block.shape[dim]
    low = lax.ppermute(lax.slice_in_dim(block, size - width, None, axis=dim), axis, forward)
    up = lax.ppermute(lax.slice_in_dim(block, 0, width, axis=dim), axis, backward)
    return jnp.concatenate([low, block, up], axis=dim)


def advance(phi, u, v, band):
    center = phi[1:-1, 1:-1]
    back_x = center - phi[:-2, 1:-1]
    ahead_x = phi[2:, 1:-1] - center
    back_y = center - phi[1:-1, :-2]
    ahead_y = phi[1:-1, 2:] - center
    transport = jnp.maximum(u, 0.0) * back_x + jnp.minimum(u, 0.0) * ahead_x
    transport = transport + jnp.maximum(v, 0.0) * back_y + jnp.minimum(v, 0.0) * ahead_y
    return center - time_step * band * transport


MESH = pl.DeviceIdType.MESH
f32 = jnp.float32
NT = (((1,), (1,)), ((), ()))
NN = (((1,), (0,)), ((), ()))
CW = 256


def split(x):
    hi = x.astype(jnp.bfloat16)
    return hi, (x - hi.astype(f32)).astype(jnp.bfloat16)


def np_split(x):
    x = x.astype(np.float32)
    hi = x.astype(jnp.bfloat16)
    lo = (x - hi.astype(np.float32)).astype(jnp.bfloat16)
    return jnp.asarray(hi), jnp.asarray(lo)


def dot3(a, b, dims):
    def one(x, y):
        return lax.dot_general(x, y, dims, preferred_element_type=f32)

    return one(a[0], b[0]) + (one(a[0], b[1]) + one(a[1], b[0]))


def spread(R, me, src, dst, send, recv):
    chan = lax.axis_index("chan")
    copies = []
    for step in range(1, R):
        to = lax.rem(me + step, R)
        copies.append(
            pltpu.make_async_remote_copy(
                src_ref=src.at[to],
                dst_ref=dst.at[me],
                send_sem=send.at[step],
                recv_sem=recv.at[step],
                device_id=(to, chan),
                device_id_type=MESH,
            )
        )
    return copies


def greet(R, me, chan):
    barrier = pltpu.get_barrier_semaphore()
    for step in range(1, R):
        pl.semaphore_signal(
            barrier, inc=1, device_id=(lax.rem(me + step, R), chan), device_id_type=MESH
        )
    pl.semaphore_signal(barrier, inc=1, device_id=(me, 1 - chan), device_id_type=MESH)
    return barrier


def forward_kernel(R, hid, fyh, fyl, txh, txl, out, spec, got, xs, chs, chr_, ssem, rsem, csem):
    me = lax.axis_index("rows")
    chan = lax.axis_index("chan")
    cl, rc, ny = hid.shape
    barrier = greet(R, me, chan)
    acc = jnp.zeros((fyh.shape[0], cl * rc), f32)
    kc = 512
    for j in range(ny // kc):
        cols = slice(j * kc, (j + 1) * kc)
        h = split(hid[:, :, cols].reshape(cl * rc, kc))
        acc = acc + dot3((fyh[:, cols], fyl[:, cols]), h, NT)
    spec[...] = acc.reshape(spec.shape)
    pl.semaphore_wait(barrier, R)
    copies = spread(R, me, spec, got, ssem, rsem)
    for copy in copies:
        copy.start()
    got[me] = spec[me]
    for copy in copies:
        copy.wait()
    half = cl * 8
    for ri in range(2):
        for c in range(cl):
            xs[ri * half + c * 8 : ri * half + c * 8 + 8, :] = jnp.concatenate(
                [got[s, ri * 8 : ri * 8 + 8, c * rc : (c + 1) * rc] for s in range(R)], axis=1
            )
    g = dot3((txh[...], txl[...]), split(xs[...]), NT)
    mx = g.shape[0] // 2
    re = g[:mx, :half] + g[mx:, half:]
    im = g[:mx, half:] - g[mx:, :half]
    hp = mx // 2
    for d in range(2):
        chs[d, 0] = re[d * hp : (d + 1) * hp]
        chs[d, 1] = im[d * hp : (d + 1) * hp]
    copy = pltpu.make_async_remote_copy(
        src_ref=chs.at[1 - chan],
        dst_ref=chr_,
        send_sem=csem.at[0],
        recv_sem=csem.at[1],
        device_id=(me, 1 - chan),
        device_id_type=MESH,
    )
    copy.start()
    out[chan] = chs[chan]
    copy.wait()
    out[1 - chan] = chr_[...]


def inverse_kernel(
    R, hid, mixd, tih, til, iyh, iyl, gain, bias, pw, pb, mask, front, flags,
    vel, nxt,
    mall, chr_, isrc, igot, xs, xth, xtl, spc, psend, pgot, own, phi, ab,
    ssem, rsem, csem, psem, qsem, hs, hr,
):
    me = lax.axis_index("rows")
    chan = lax.axis_index("chan")
    cl, rc, ny = hid.shape
    half = cl * 8
    tw = ny // 2
    nch = tw // CW
    last = R - 1
    phi[...] = jnp.zeros_like(phi)
    ab[...] = jnp.zeros_like(ab)
    phi[8 : 8 + rc, 128 : 128 + tw] = front[...]
    barrier = greet(R, me, chan)

    for step in (1, R - 1):
        pl.semaphore_signal(
            barrier, inc=1, device_id=(lax.rem(me + step, R), 1 - chan), device_id_type=MESH
        )
    pl.semaphore_wait(barrier, R + 2)

    ccopy = pltpu.make_async_remote_copy(
        src_ref=mixd.at[1 - chan],
        dst_ref=chr_,
        send_sem=csem.at[0],
        recv_sem=csem.at[1],
        device_id=(me, 1 - chan),
        device_id_type=MESH,
    )
    ccopy.start()

    csrc = pl.multiple_of(tw - (tw - 128) * chan, 128)
    cdst = pl.multiple_of((tw + 128) * chan, 128)
    mid = (pl.ds(128, tw), pl.ds(128, tw))
    side = (pl.ds(csrc, 128), pl.ds(cdst, 128))
    up = (pl.ds(8, 8), pl.ds(8 + rc, 8))
    down = (pl.ds(rc, 8), pl.ds(0, 8))
    level = (pl.ds(8, rc), pl.ds(8, rc))
    moves = [(-1, 0, up, mid), (1, 0, down, mid), (0, 1, level, side), (-1, 1, up, side), (1, 1, down, side)]

    def halo(which, ref, act):
        for n, (dr, dc, rows, cols) in enumerate(moves):
            i = which * 5 + n
            lead = () if which == 0 else (slice(None),)
            copy = pltpu.make_async_remote_copy(
                src_ref=ref.at[lead + (rows[0], cols[0])],
                dst_ref=ref.at[lead + (rows[1], cols[1])],
                send_sem=hs.at[i],
                recv_sem=hr.at[i],
                device_id=(me + dr, 1 - chan if dc else chan),
                device_id_type=MESH,
            )
            first = (lambda: copy.start()) if act == "start" else (lambda: copy.wait_send())
            if dr == 0:
                first()
                if act == "wait":
                    copy.wait_recv()
            else:
                pl.when(me > 0 if dr < 0 else me < last)(first)
                if act == "wait":
                    pl.when(me < last if dr < 0 else me > 0)(lambda: copy.wait_recv())

    halo(0, phi, "start")

    mall[chan] = mixd[chan]
    ccopy.wait()
    mall[1 - chan] = chr_[...]
    re = jnp.concatenate([mall[0, 0], mall[1, 0]], axis=0)
    im = jnp.concatenate([mall[0, 1], mall[1, 1]], axis=0)
    full = jnp.concatenate(
        [jnp.concatenate([re, im], axis=1), jnp.concatenate([-im, re], axis=1)], axis=0
    )
    res = dot3((tih[...], til[...]), split(full), NN)
    isrc[...] = res.reshape(isrc.shape)
    copies = spread(R, me, isrc, igot, ssem, rsem)
    for copy in copies:
        copy.start()
    igot[me] = isrc[me]
    for copy in copies:
        copy.wait()
    for s in range(R):
        t = igot[s].T
        for ri in range(2):
            xs[s * 16 + ri * 8 : s * 16 + ri * 8 + 8, :] = jnp.concatenate(
                [t[ri * half + c * 8 : ri * half + c * 8 + 8, :] for c in range(cl)], axis=1
            )
    xt = split(xs[...].T)
    xth[...] = xt[0]
    xtl[...] = xt[1]

    def share(col):
        cols = pl.ds(pl.multiple_of(col, CW), CW)
        spc[...] = dot3((xth[...], xtl[...]), (iyh[:, cols], iyl[:, cols]), NN)
        u = jnp.zeros((rc, CW), f32)
        v = jnp.zeros((rc, CW), f32)
        for c in range(cl):
            z = spc[c * rc : (c + 1) * rc, :] + (gain[c] * hid[c, :, cols] + bias[c])
            a = (0.5 * z) * (1.0 + lax.erf(z * (0.5**0.5)))
            u = u + pw[0, c] * a
            v = v + pw[1, c] * a
        return u, v

    def pcopy(j):
        return pltpu.make_async_remote_copy(
            src_ref=psend.at[j],
            dst_ref=pgot.at[j],
            send_sem=psem.at[j],
            recv_sem=qsem.at[j],
            device_id=(me, 1 - chan),
            device_id_type=MESH,
        )

    def theirs(j, carry):
        u, v = share((1 - chan) * tw + j * CW)
        psend[j, 0] = u
        psend[j, 1] = v
        pcopy(j).start()
        return carry

    def ours(j, carry):
        u, v = share(chan * tw + j * CW)
        own[j, 0] = u
        own[j, 1] = v
        return carry

    lax.fori_loop(0, nch, theirs, 0)
    lax.fori_loop(0, nch, ours, 0)
    for j in range(nch):
        pcopy(j).wait()
        cols = slice(j * CW, (j + 1) * CW)
        ice = mask[:, cols].astype(f32)
        band = flags[:, cols].astype(f32) * time_step
        for k in range(2):
            w = (own[j, k] + pgot[j, k] + pb[k]) * ice
            vel[k, :, cols] = w
            ab[k, 8 : 8 + rc, 128 + j * CW : 128 + (j + 1) * CW] = w * band
    halo(1, ab, "start")
    halo(0, phi, "wait")
    halo(1, ab, "wait")
    a = ab[0]
    b = ab[1]
    ap, am = jnp.maximum(a, 0.0), jnp.minimum(a, 0.0)
    bp, bm = jnp.maximum(b, 0.0), jnp.minimum(b, 0.0)
    x = phi[...]
    nr, nc = x.shape
    for _ in range(LS_STEPS):
        move = ap * (x - pltpu.roll(x, 1, 0)) + am * (pltpu.roll(x, nr - 1, 0) - x)
        move = move + (bp * (x - pltpu.roll(x, 1, 1)) + bm * (pltpu.roll(x, nc - 1, 1) - x))
        x = x - move
    nxt[...] = x[8 : 8 + rc, 128 : 128 + tw]


def on_kernels(
    hidden, front, spectral_weight, skip_gain, skip_bias, project_weight, project_bias,
    ice_mask, front_flags,
):
    cl, rc, ny = hidden.shape
    R = lax.axis_size("rows")
    D = lax.axis_size("chan")
    ql = spectral_weight.shape[1]
    pn = spectral_weight.shape[2]
    nx, mx, my = rc * R, pn * D, ql * R
    scale = 1.0 / math.sqrt(nx * ny * mx * my)
    yph = np_angles(np.arange(my), np.arange(ny), ny).reshape(R, ql, ny)
    fy = np.stack([np.cos(yph), -np.sin(yph)], axis=1).reshape(2 * my, ny)
    w = np.where(np.arange(my) == 0, 1.0, 2.0).reshape(R, ql, 1) * scale
    iy = np.stack([w * np.cos(yph), -w * np.sin(yph)], axis=1).reshape(2 * my, ny)
    pid = np.arange(mx)
    xph = np_angles(np.where(pid < mx // 2, pid, pid - mx), np.arange(nx), nx)
    tx = np.concatenate([np.cos(xph), np.sin(xph)], axis=0)
    vm = pl.BlockSpec(memory_space=pltpu.VMEM)
    sm = pl.BlockSpec(memory_space=pltpu.SMEM)
    dma = pltpu.SemaphoreType.DMA
    lanes = cl * ql

    def kernel_a(*refs):
        forward_kernel(R, *refs)

    def kernel_b(*refs):
        inverse_kernel(R, *refs)

    spec = pl.pallas_call(
        kernel_a,
        out_shape=jax.ShapeDtypeStruct((D, 2, pn, lanes), f32),
        in_specs=[vm] * 5,
        out_specs=vm,
        scratch_shapes=[
            pltpu.VMEM((R, 2 * ql, cl * rc), f32),
            pltpu.VMEM((R, 2 * ql, cl * rc), f32),
            pltpu.VMEM((2 * lanes, nx), f32),
            pltpu.VMEM((D, 2, pn, lanes), f32),
            pltpu.VMEM((2, pn, lanes), f32),
            dma((R,)),
            dma((R,)),
            dma((2,)),
        ],
        compiler_params=pltpu.CompilerParams(
            collective_id=0, has_side_effects=True, vmem_limit_bytes=40 * 2**20
        ),
        name="forward",
    )(hidden, *np_split(fy), *np_split(tx))
    spec = spec.reshape(D, 2, pn, cl, ql).transpose(1, 0, 3, 4, 2).reshape(2, D * cl, ql, pn)
    wt = spectral_weight.transpose(0, 3, 4, 1, 2)
    a, b = spec[0][:, None], spec[1][:, None]
    re = jnp.sum(wt[0] * a - wt[1] * b, axis=0)
    im = jnp.sum(wt[0] * b + wt[1] * a, axis=0)
    mixed = jnp.stack([re, im]).reshape(2, D, cl, ql, pn).transpose(1, 0, 4, 2, 3)
    mixed = mixed.reshape(D, 2, pn, lanes)
    nch = ny // D // CW
    tw = ny // D
    return pl.pallas_call(
        kernel_b,
        out_shape=(
            jax.ShapeDtypeStruct((2, rc, tw), f32),
            jax.ShapeDtypeStruct((rc, tw), f32),
        ),
        in_specs=[vm] * 6 + [sm] * 4 + [vm] * 3,
        out_specs=(vm, vm),
        scratch_shapes=[
            pltpu.VMEM((D, 2, pn, lanes), f32),
            pltpu.VMEM((2, pn, lanes), f32),
            pltpu.VMEM((R, rc, 2 * lanes), f32),
            pltpu.VMEM((R, rc, 2 * lanes), f32),
            pltpu.VMEM((2 * my, cl * rc), f32),
            pltpu.VMEM((cl * rc, 2 * my), jnp.bfloat16),
            pltpu.VMEM((cl * rc, 2 * my), jnp.bfloat16),
            pltpu.VMEM((cl * rc, CW), f32),
            pltpu.VMEM((nch, 2, rc, CW), f32),
            pltpu.VMEM((nch, 2, rc, CW), f32),
            pltpu.VMEM((nch, 2, rc, CW), f32),
            pltpu.VMEM((rc + 16, tw + 256), f32),
            pltpu.VMEM((2, rc + 16, tw + 256), f32),
            dma((R,)),
            dma((R,)),
            dma((2,)),
            dma((nch,)),
            dma((nch,)),
            dma((10,)),
            dma((10,)),
        ],
        compiler_params=pltpu.CompilerParams(
            collective_id=1, has_side_effects=True, vmem_limit_bytes=40 * 2**20
        ),
        name="inverse",
    )(
        hidden, mixed, *np_split(tx.T), *np_split(iy), skip_gain, skip_bias,
        project_weight, project_bias, ice_mask, front, front_flags,
    )


def on_device(
    hidden,
    front,
    spectral_weight,
    skip_gain,
    skip_bias,
    project_weight,
    project_bias,
    ice_mask,
    front_flags,
):
    cl, rc, ny = hidden.shape
    R = lax.axis_size("rows")
    D = lax.axis_size("chan")
    ql = spectral_weight.shape[1]
    if D == 2 and ql == 8 and cl * ql == 128 and rc % 8 == 0 and (rc * R) % 128 == 0:
        return on_kernels(
            hidden, front, spectral_weight, skip_gain, skip_bias, project_weight,
            project_bias, ice_mask, front_flags,
        )
    pl_ = spectral_weight.shape[2]
    nx = rc * R
    mx = pl_ * D
    my = ql * R
    scale = 1.0 / math.sqrt(nx * ny * mx * my)
    yph = np_angles(np.arange(my), np.arange(ny), ny)
    fy = np.stack([np.cos(yph), -np.sin(yph)], axis=1).reshape(2 * my, ny).astype(np.float32)
    w = np.where(np.arange(my) == 0, 1.0, 2.0)[:, None] * scale
    iy = np.stack([w * np.cos(yph), -w * np.sin(yph)], axis=1).reshape(2 * my, ny).astype(np.float32)
    pid = np.arange(mx)
    kp = np.where(pid < mx // 2, pid, pid - mx)
    xph = np_angles(kp, np.arange(nx), nx)
    cx = np.cos(xph).astype(np.float32)
    sx = np.sin(xph).astype(np.float32)
    fx = np.stack([np.stack([cx, -sx]), np.stack([sx, cx])]).transpose(0, 3, 1, 2).reshape(2, nx, 2 * mx)
    ix = np.stack([np.stack([cx, sx]), np.stack([-sx, cx])]).reshape(2, 2, mx, nx)

    spec_y = jnp.einsum("ky,cxy->kcx", jnp.asarray(fy), hidden, precision=high)
    recv = lax.all_to_all(spec_y.reshape(R, ql, 2, cl, rc), "rows", 0, 0, tiled=True)
    spec = jnp.einsum(
        "sqrcx,rsxP->qcP", recv, jnp.asarray(fx).reshape(2, R, rc, 2 * mx), precision=high
    ).reshape(ql, cl, 2, D, pl_)
    spec = lax.all_to_all(spec.transpose(3, 1, 2, 0, 4), "chan", 0, 0, tiled=True)
    spec = spec.reshape(D * cl, 2, ql, pl_)
    wt = spectral_weight.transpose(0, 3, 4, 1, 2)
    a, b = spec[:, 0][:, None], spec[:, 1][:, None]
    re = jnp.sum(wt[0] * a - wt[1] * b, axis=0)
    im = jnp.sum(wt[0] * b + wt[1] * a, axis=0)
    mixed = jnp.stack([re, im], axis=1).reshape(D, cl, 2, ql, pl_)
    mixed = lax.all_to_all(mixed, "chan", 0, 0, tiled=True)
    inv = jnp.einsum(
        "dcrqp,rtdpx->xqtc", mixed, jnp.asarray(ix).reshape(2, 2, D, pl_, nx), precision=high
    ).transpose(1, 2, 3, 0).reshape(ql, 2, cl, R, rc)
    inv = lax.all_to_all(inv.transpose(3, 0, 1, 2, 4), "rows", 0, 0, tiled=True)
    inv = inv.reshape(2 * my, cl, rc)
    spectral = jnp.einsum("kcx,ky->cxy", inv, jnp.asarray(iy), precision=high)
    act = jax.nn.gelu(
        spectral + skip_gain[:, None, None] * hidden + skip_bias[:, None, None], approximate=False
    )
    part = jnp.stack(
        [jnp.sum(project_weight[j][:, None, None] * act, axis=0) for j in range(2)]
    )
    part = part.reshape(2, rc, D, ny // D).transpose(2, 0, 1, 3)
    got = lax.all_to_all(part, "chan", 0, 0, tiled=True)
    speed = jnp.sum(got, axis=0) + project_bias[:, None, None]
    velocity = speed * ice_mask.astype(jnp.float32)[None]
    band = front_flags.astype(jnp.float32)
    W = LS_STEPS
    state = jnp.concatenate([velocity, band[None], front[None]], axis=0)
    state = with_halo(with_halo(state, "rows", 1, W), "chan", 2, W)
    u, v, bd, level = state[0], state[1], state[2], state[3]
    for step in range(LS_STEPS):
        i = step + 1
        level = advance(level, u[i:-i, i:-i], v[i:-i, i:-i], bd[i:-i, i:-i])
    return (velocity, level)


def solution(mesh):
    return jax.shard_map(
        on_device,
        mesh=mesh,
        in_specs=(
            P("chan", "rows", None),
            P("rows", "chan"),
            P(None, "rows", "chan", None, None),
            P("chan"),
            P("chan"),
            P(None, "chan"),
            P(),
            P("rows", "chan"),
            P("rows", "chan"),
        ),
        out_specs=(P(None, "rows", "chan"), P("rows", "chan")),
        check_vma=False,
    )
```

```python
import math

import jax
import jax.numpy as jnp
import numpy as np
from jax import lax
from jax.experimental import pallas as pl
from jax.experimental.pallas import tpu as pltpu
from jax.sharding import PartitionSpec as P

LS_STEPS = 4
time_step = 0.25
high = lax.Precision.HIGH


def np_angles(freqs, places, length):
    return 2.0 * math.pi / length * ((freqs[:, None] * places[None, :]) % length)


def with_halo(block, axis, dim, width):
    count = lax.axis_size(axis)
    forward = [(i, i + 1) for i in range(count - 1)]
    backward = [(target, source) for source, target in forward]
    size = block.shape[dim]
    low = lax.ppermute(lax.slice_in_dim(block, size - width, None, axis=dim), axis, forward)
    up = lax.ppermute(lax.slice_in_dim(block, 0, width, axis=dim), axis, backward)
    return jnp.concatenate([low, block, up], axis=dim)


def advance(phi, u, v, band):
    center = phi[1:-1, 1:-1]
    back_x = center - phi[:-2, 1:-1]
    ahead_x = phi[2:, 1:-1] - center
    back_y = center - phi[1:-1, :-2]
    ahead_y = phi[1:-1, 2:] - center
    transport = jnp.maximum(u, 0.0) * back_x + jnp.minimum(u, 0.0) * ahead_x
    transport = transport + jnp.maximum(v, 0.0) * back_y + jnp.minimum(v, 0.0) * ahead_y
    return center - time_step * band * transport


MESH = pl.DeviceIdType.MESH
f32 = jnp.float32
NT = (((1,), (1,)), ((), ()))
NN = (((1,), (0,)), ((), ()))
CW = 256


def split(x):
    hi = x.astype(jnp.bfloat16)
    return hi, (x - hi.astype(f32)).astype(jnp.bfloat16)


def np_split(x):
    x = x.astype(np.float32)
    hi = x.astype(jnp.bfloat16)
    lo = (x - hi.astype(np.float32)).astype(jnp.bfloat16)
    return jnp.asarray(hi), jnp.asarray(lo)


def dot3(a, b, dims):
    def one(x, y):
        return lax.dot_general(x, y, dims, preferred_element_type=f32)

    return one(a[0], b[0]) + (one(a[0], b[1]) + one(a[1], b[0]))


def spread(R, me, half, src, dst, send, recv):
    chan = lax.axis_index("chan")
    copies = []
    for step in range(1, R):
        to = lax.rem(me + step, R)
        copies.append(
            pltpu.make_async_remote_copy(
                src_ref=src.at[half, to],
                dst_ref=dst.at[half, me],
                send_sem=send.at[half * R + step],
                recv_sem=recv.at[half * R + step],
                device_id=(to, chan),
                device_id_type=MESH,
            )
        )
    return copies


def greet(R, me, chan):
    barrier = pltpu.get_barrier_semaphore()
    for step in range(1, R):
        pl.semaphore_signal(
            barrier, inc=1, device_id=(lax.rem(me + step, R), chan), device_id_type=MESH
        )
    pl.semaphore_signal(barrier, inc=1, device_id=(me, 1 - chan), device_id_type=MESH)
    return barrier


def forward_kernel(
    R, hid_in, fyh_in, fyl_in, txh_in, txl_in, out,
    hid, fyh, fyl, txh, txl, spec, got, xs, chs, chr_, ssem, rsem, csem, lsem,
):
    me = lax.axis_index("rows")
    chan = lax.axis_index("chan")
    cl, rc, ny = hid.shape
    ch = cl // 2
    pairs = [
        (fyh_in, fyh),
        (hid_in.at[pl.ds(0, ch)], hid.at[pl.ds(0, ch)]),
        (fyl_in, fyl),
        (hid_in.at[pl.ds(ch, ch)], hid.at[pl.ds(ch, ch)]),
        (txh_in, txh),
        (txl_in, txl),
    ]
    loads = [pltpu.make_async_copy(a, b, lsem.at[n]) for n, (a, b) in enumerate(pairs)]
    for load in loads:
        load.start()
    barrier = greet(R, me, chan)
    kc = 512
    half = cl * 8
    sent = []
    for h in range(2):
        for load in loads[0:3] if h == 0 else loads[3:4]:
            load.wait()
        acc = jnp.zeros((fyh.shape[0], ch * rc), f32)
        for j in range(ny // kc):
            cols = slice(j * kc, (j + 1) * kc)
            x = split(hid[h * ch : (h + 1) * ch, :, cols].reshape(ch * rc, kc))
            acc = acc + dot3((fyh[:, cols], fyl[:, cols]), x, NT)
        spec[h] = acc.reshape(spec.shape[1:])
        if h == 0:
            pl.semaphore_wait(barrier, R)
        copies = spread(R, me, h, spec, got, ssem, rsem)
        for copy in copies:
            copy.start()
        got[h, me] = spec[h, me]
        sent.append(copies)
    for h in range(2):
        for copy in sent[h]:
            copy.wait()
        for ri in range(2):
            for c in range(ch):
                at = ri * half + (h * ch + c) * 8
                xs[at : at + 8, :] = jnp.concatenate(
                    [got[h, s, ri * 8 : ri * 8 + 8, c * rc : (c + 1) * rc] for s in range(R)],
                    axis=1,
                )
    for load in loads[4:]:
        load.wait()
    g = dot3((txh[...], txl[...]), split(xs[...]), NT)
    mx = g.shape[0] // 2
    re = g[:mx, :half] + g[mx:, half:]
    im = g[:mx, half:] - g[mx:, :half]
    hp = mx // 2
    for d in range(2):
        chs[d, 0] = re[d * hp : (d + 1) * hp]
        chs[d, 1] = im[d * hp : (d + 1) * hp]
    copy = pltpu.make_async_remote_copy(
        src_ref=chs.at[1 - chan],
        dst_ref=chr_,
        send_sem=csem.at[0],
        recv_sem=csem.at[1],
        device_id=(me, 1 - chan),
        device_id_type=MESH,
    )
    copy.start()
    out[chan] = chs[chan]
    copy.wait()
    out[1 - chan] = chr_[...]


def inverse_kernel(
    R, hid_in, mixd, tih, til, iyh, iyl, gain, bias, pw, pb, mask, front, flags,
    vel, nxt,
    mall, chr_, isrc, igot, xs, xth, xtl, spc, psend, pgot, own, phi, ab,
    ssem, rsem, csem, psem, qsem, hs, hr, hid, lsem,
):
    me = lax.axis_index("rows")
    chan = lax.axis_index("chan")
    cl, rc, ny = hid.shape
    half = cl * 8
    tw = ny // 2
    rh = rc // 2
    load = pltpu.make_async_copy(hid_in, hid, lsem.at[0])
    load.start()
    nch = tw // CW
    last = R - 1
    phi[...] = jnp.zeros_like(phi)
    ab[...] = jnp.zeros_like(ab)
    phi[8 : 8 + rc, 128 : 128 + tw] = front[...]
    barrier = greet(R, me, chan)

    for step in (1, R - 1):
        pl.semaphore_signal(
            barrier, inc=1, device_id=(lax.rem(me + step, R), 1 - chan), device_id_type=MESH
        )
    pl.semaphore_wait(barrier, R + 2)

    ccopy = pltpu.make_async_remote_copy(
        src_ref=mixd.at[1 - chan],
        dst_ref=chr_,
        send_sem=csem.at[0],
        recv_sem=csem.at[1],
        device_id=(me, 1 - chan),
        device_id_type=MESH,
    )
    ccopy.start()

    csrc = pl.multiple_of(tw - (tw - 128) * chan, 128)
    cdst = pl.multiple_of((tw + 128) * chan, 128)
    mid = (pl.ds(128, tw), pl.ds(128, tw))
    side = (pl.ds(csrc, 128), pl.ds(cdst, 128))
    up = (pl.ds(8, 8), pl.ds(8 + rc, 8))
    down = (pl.ds(rc, 8), pl.ds(0, 8))
    level = (pl.ds(8, rc), pl.ds(8, rc))
    moves = [(-1, 0, up, mid), (1, 0, down, mid), (0, 1, level, side), (-1, 1, up, side), (1, 1, down, side)]

    def halo(which, ref, act):
        for n, (dr, dc, rows, cols) in enumerate(moves):
            i = which * 5 + n
            lead = () if which == 0 else (slice(None),)
            copy = pltpu.make_async_remote_copy(
                src_ref=ref.at[lead + (rows[0], cols[0])],
                dst_ref=ref.at[lead + (rows[1], cols[1])],
                send_sem=hs.at[i],
                recv_sem=hr.at[i],
                device_id=(me + dr, 1 - chan if dc else chan),
                device_id_type=MESH,
            )
            first = (lambda: copy.start()) if act == "start" else (lambda: copy.wait_send())
            if dr == 0:
                first()
                if act == "wait":
                    copy.wait_recv()
            else:
                pl.when(me > 0 if dr < 0 else me < last)(first)
                if act == "wait":
                    pl.when(me < last if dr < 0 else me > 0)(lambda: copy.wait_recv())

    halo(0, phi, "start")

    mall[chan] = mixd[chan]
    ccopy.wait()
    mall[1 - chan] = chr_[...]
    re = jnp.concatenate([mall[0, 0], mall[1, 0]], axis=0)
    im = jnp.concatenate([mall[0, 1], mall[1, 1]], axis=0)
    full = jnp.concatenate(
        [jnp.concatenate([re, im], axis=1), jnp.concatenate([-im, re], axis=1)], axis=0
    )
    res = dot3((tih[...], til[...]), split(full), NN)
    res = res.reshape(R, 2, rh, 2 * half)
    sent = []
    for h in range(2):
        isrc[h] = res[:, h]
        copies = spread(R, me, h, isrc, igot, ssem, rsem)
        for copy in copies:
            copy.start()
        igot[h, me] = isrc[h, me]
        sent.append(copies)

    def share(h, col):
        cols = pl.ds(pl.multiple_of(col, CW), CW)
        spc[...] = dot3((xth[...], xtl[...]), (iyh[:, cols], iyl[:, cols]), NN)
        u = jnp.zeros((rh, CW), f32)
        v = jnp.zeros((rh, CW), f32)
        for c in range(cl):
            skip = gain[c] * hid[c, h * rh : (h + 1) * rh, cols] + bias[c]
            z = spc[c * rh : (c + 1) * rh, :] + skip
            a = (0.5 * z) * (1.0 + lax.erf(z * (0.5**0.5)))
            u = u + pw[0, c] * a
            v = v + pw[1, c] * a
        return u, v

    def pcopy(h, j):
        return pltpu.make_async_remote_copy(
            src_ref=psend.at[h, j],
            dst_ref=pgot.at[h, j],
            send_sem=psem.at[h * nch + j],
            recv_sem=qsem.at[h * nch + j],
            device_id=(me, 1 - chan),
            device_id_type=MESH,
        )

    for h in range(2):
        for copy in sent[h]:
            copy.wait()
        for s in range(R):
            t = igot[h, s].T
            for ri in range(2):
                xs[s * 16 + ri * 8 : s * 16 + ri * 8 + 8, :] = jnp.concatenate(
                    [t[ri * half + c * 8 : ri * half + c * 8 + 8, :] for c in range(cl)], axis=1
                )
        xt = split(xs[...].T)
        xth[...] = xt[0]
        xtl[...] = xt[1]
        if h == 0:
            load.wait()

        def theirs(j, carry):
            u, v = share(h, (1 - chan) * tw + j * CW)
            psend[h, j, 0] = u
            psend[h, j, 1] = v
            pcopy(h, j).start()
            return carry

        def ours(j, carry):
            u, v = share(h, chan * tw + j * CW)
            own[h, j, 0] = u
            own[h, j, 1] = v
            return carry

        lax.fori_loop(0, nch, theirs, 0)
        lax.fori_loop(0, nch, ours, 0)
    for h in range(2):
        rows = slice(h * rh, (h + 1) * rh)
        for j in range(nch):
            pcopy(h, j).wait()
            cols = slice(j * CW, (j + 1) * CW)
            ice = mask[rows, cols].astype(f32)
            band = flags[rows, cols].astype(f32) * time_step
            for k in range(2):
                w = (own[h, j, k] + pgot[h, j, k] + pb[k]) * ice
                vel[k, rows, cols] = w
                ab[k, 8 + h * rh : 8 + (h + 1) * rh, 128 + j * CW : 128 + (j + 1) * CW] = w * band
    halo(1, ab, "start")
    halo(0, phi, "wait")
    halo(1, ab, "wait")
    a = ab[0]
    b = ab[1]
    ap, am = jnp.maximum(a, 0.0), jnp.minimum(a, 0.0)
    bp, bm = jnp.maximum(b, 0.0), jnp.minimum(b, 0.0)
    x = phi[...]
    nr, nc = x.shape
    for _ in range(LS_STEPS):
        move = ap * (x - pltpu.roll(x, 1, 0)) + am * (pltpu.roll(x, nr - 1, 0) - x)
        move = move + (bp * (x - pltpu.roll(x, 1, 1)) + bm * (pltpu.roll(x, nc - 1, 1) - x))
        x = x - move
    nxt[...] = x[8 : 8 + rc, 128 : 128 + tw]


def on_kernels(
    hidden, front, spectral_weight, skip_gain, skip_bias, project_weight, project_bias,
    ice_mask, front_flags,
):
    cl, rc, ny = hidden.shape
    R = lax.axis_size("rows")
    D = lax.axis_size("chan")
    ql = spectral_weight.shape[1]
    pn = spectral_weight.shape[2]
    nx, mx, my = rc * R, pn * D, ql * R
    scale = 1.0 / math.sqrt(nx * ny * mx * my)
    yph = np_angles(np.arange(my), np.arange(ny), ny).reshape(R, ql, ny)
    fy = np.stack([np.cos(yph), -np.sin(yph)], axis=1).reshape(2 * my, ny)
    w = np.where(np.arange(my) == 0, 1.0, 2.0).reshape(R, ql, 1) * scale
    iy = np.stack([w * np.cos(yph), -w * np.sin(yph)], axis=1).reshape(2 * my, ny)
    pid = np.arange(mx)
    xph = np_angles(np.where(pid < mx // 2, pid, pid - mx), np.arange(nx), nx)
    tx = np.concatenate([np.cos(xph), np.sin(xph)], axis=0)
    vm = pl.BlockSpec(memory_space=pltpu.VMEM)
    sm = pl.BlockSpec(memory_space=pltpu.SMEM)
    hbm = pl.BlockSpec(memory_space=pltpu.HBM)
    bf16 = jnp.bfloat16
    dma = pltpu.SemaphoreType.DMA
    lanes = cl * ql

    def kernel_a(*refs):
        forward_kernel(R, *refs)

    def kernel_b(*refs):
        inverse_kernel(R, *refs)

    spec = pl.pallas_call(
        kernel_a,
        out_shape=jax.ShapeDtypeStruct((D, 2, pn, lanes), f32),
        in_specs=[hbm] * 5,
        out_specs=vm,
        scratch_shapes=[
            pltpu.VMEM((cl, rc, ny), f32),
            pltpu.VMEM((2 * my, ny), bf16),
            pltpu.VMEM((2 * my, ny), bf16),
            pltpu.VMEM((2 * mx, nx), bf16),
            pltpu.VMEM((2 * mx, nx), bf16),
            pltpu.VMEM((2, R, 2 * ql, cl // 2 * rc), f32),
            pltpu.VMEM((2, R, 2 * ql, cl // 2 * rc), f32),
            pltpu.VMEM((2 * lanes, nx), f32),
            pltpu.VMEM((D, 2, pn, lanes), f32),
            pltpu.VMEM((2, pn, lanes), f32),
            dma((2 * R,)),
            dma((2 * R,)),
            dma((2,)),
            dma((6,)),
        ],
        compiler_params=pltpu.CompilerParams(
            collective_id=0, has_side_effects=True, vmem_limit_bytes=40 * 2**20
        ),
        name="forward",
    )(hidden, *np_split(fy), *np_split(tx))
    spec = spec.reshape(D, 2, pn, cl, ql).transpose(1, 0, 3, 4, 2).reshape(2, D * cl, ql, pn)
    wt = spectral_weight.transpose(0, 3, 4, 1, 2)
    a, b = spec[0][:, None], spec[1][:, None]
    re = jnp.sum(wt[0] * a - wt[1] * b, axis=0)
    im = jnp.sum(wt[0] * b + wt[1] * a, axis=0)
    mixed = jnp.stack([re, im]).reshape(2, D, cl, ql, pn).transpose(1, 0, 4, 2, 3)
    mixed = mixed.reshape(D, 2, pn, lanes)
    nch = ny // D // CW
    tw = ny // D
    return pl.pallas_call(
        kernel_b,
        out_shape=(
            jax.ShapeDtypeStruct((2, rc, tw), f32),
            jax.ShapeDtypeStruct((rc, tw), f32),
        ),
        in_specs=[hbm] + [vm] * 5 + [sm] * 4 + [vm] * 3,
        out_specs=(vm, vm),
        scratch_shapes=[
            pltpu.VMEM((D, 2, pn, lanes), f32),
            pltpu.VMEM((2, pn, lanes), f32),
            pltpu.VMEM((2, R, rc // 2, 2 * lanes), f32),
            pltpu.VMEM((2, R, rc // 2, 2 * lanes), f32),
            pltpu.VMEM((2 * my, cl * rc // 2), f32),
            pltpu.VMEM((cl * rc // 2, 2 * my), bf16),
            pltpu.VMEM((cl * rc // 2, 2 * my), bf16),
            pltpu.VMEM((cl * rc // 2, CW), f32),
            pltpu.VMEM((2, nch, 2, rc // 2, CW), f32),
            pltpu.VMEM((2, nch, 2, rc // 2, CW), f32),
            pltpu.VMEM((2, nch, 2, rc // 2, CW), f32),
            pltpu.VMEM((rc + 16, tw + 256), f32),
            pltpu.VMEM((2, rc + 16, tw + 256), f32),
            dma((2 * R,)),
            dma((2 * R,)),
            dma((2,)),
            dma((2 * nch,)),
            dma((2 * nch,)),
            dma((10,)),
            dma((10,)),
            pltpu.VMEM((cl, rc, ny), f32),
            dma((1,)),
        ],
        compiler_params=pltpu.CompilerParams(
            collective_id=1, has_side_effects=True, vmem_limit_bytes=40 * 2**20
        ),
        name="inverse",
    )(
        hidden, mixed, *np_split(tx.T), *np_split(iy), skip_gain, skip_bias,
        project_weight, project_bias, ice_mask, front, front_flags,
    )


def on_device(
    hidden,
    front,
    spectral_weight,
    skip_gain,
    skip_bias,
    project_weight,
    project_bias,
    ice_mask,
    front_flags,
):
    cl, rc, ny = hidden.shape
    R = lax.axis_size("rows")
    D = lax.axis_size("chan")
    ql = spectral_weight.shape[1]
    if D == 2 and ql == 8 and cl * ql == 128 and rc % 16 == 0 and (rc * R) % 128 == 0:
        return on_kernels(
            hidden, front, spectral_weight, skip_gain, skip_bias, project_weight,
            project_bias, ice_mask, front_flags,
        )
    pl_ = spectral_weight.shape[2]
    nx = rc * R
    mx = pl_ * D
    my = ql * R
    scale = 1.0 / math.sqrt(nx * ny * mx * my)
    yph = np_angles(np.arange(my), np.arange(ny), ny)
    fy = np.stack([np.cos(yph), -np.sin(yph)], axis=1).reshape(2 * my, ny).astype(np.float32)
    w = np.where(np.arange(my) == 0, 1.0, 2.0)[:, None] * scale
    iy = np.stack([w * np.cos(yph), -w * np.sin(yph)], axis=1).reshape(2 * my, ny).astype(np.float32)
    pid = np.arange(mx)
    kp = np.where(pid < mx // 2, pid, pid - mx)
    xph = np_angles(kp, np.arange(nx), nx)
    cx = np.cos(xph).astype(np.float32)
    sx = np.sin(xph).astype(np.float32)
    fx = np.stack([np.stack([cx, -sx]), np.stack([sx, cx])]).transpose(0, 3, 1, 2).reshape(2, nx, 2 * mx)
    ix = np.stack([np.stack([cx, sx]), np.stack([-sx, cx])]).reshape(2, 2, mx, nx)

    spec_y = jnp.einsum("ky,cxy->kcx", jnp.asarray(fy), hidden, precision=high)
    recv = lax.all_to_all(spec_y.reshape(R, ql, 2, cl, rc), "rows", 0, 0, tiled=True)
    spec = jnp.einsum(
        "sqrcx,rsxP->qcP", recv, jnp.asarray(fx).reshape(2, R, rc, 2 * mx), precision=high
    ).reshape(ql, cl, 2, D, pl_)
    spec = lax.all_to_all(spec.transpose(3, 1, 2, 0, 4), "chan", 0, 0, tiled=True)
    spec = spec.reshape(D * cl, 2, ql, pl_)
    wt = spectral_weight.transpose(0, 3, 4, 1, 2)
    a, b = spec[:, 0][:, None], spec[:, 1][:, None]
    re = jnp.sum(wt[0] * a - wt[1] * b, axis=0)
    im = jnp.sum(wt[0] * b + wt[1] * a, axis=0)
    mixed = jnp.stack([re, im], axis=1).reshape(D, cl, 2, ql, pl_)
    mixed = lax.all_to_all(mixed, "chan", 0, 0, tiled=True)
    inv = jnp.einsum(
        "dcrqp,rtdpx->xqtc", mixed, jnp.asarray(ix).reshape(2, 2, D, pl_, nx), precision=high
    ).transpose(1, 2, 3, 0).reshape(ql, 2, cl, R, rc)
    inv = lax.all_to_all(inv.transpose(3, 0, 1, 2, 4), "rows", 0, 0, tiled=True)
    inv = inv.reshape(2 * my, cl, rc)
    spectral = jnp.einsum("kcx,ky->cxy", inv, jnp.asarray(iy), precision=high)
    act = jax.nn.gelu(
        spectral + skip_gain[:, None, None] * hidden + skip_bias[:, None, None], approximate=False
    )
    part = jnp.stack(
        [jnp.sum(project_weight[j][:, None, None] * act, axis=0) for j in range(2)]
    )
    part = part.reshape(2, rc, D, ny // D).transpose(2, 0, 1, 3)
    got = lax.all_to_all(part, "chan", 0, 0, tiled=True)
    speed = jnp.sum(got, axis=0) + project_bias[:, None, None]
    velocity = speed * ice_mask.astype(jnp.float32)[None]
    band = front_flags.astype(jnp.float32)
    W = LS_STEPS
    state = jnp.concatenate([velocity, band[None], front[None]], axis=0)
    state = with_halo(with_halo(state, "rows", 1, W), "chan", 2, W)
    u, v, bd, level = state[0], state[1], state[2], state[3]
    for step in range(LS_STEPS):
        i = step + 1
        level = advance(level, u[i:-i, i:-i], v[i:-i, i:-i], bd[i:-i, i:-i])
    return (velocity, level)


def solution(mesh):
    return jax.shard_map(
        on_device,
        mesh=mesh,
        in_specs=(
            P("chan", "rows", None),
            P("rows", "chan"),
            P(None, "rows", "chan", None, None),
            P("chan"),
            P("chan"),
            P(None, "chan"),
            P(),
            P("rows", "chan"),
            P("rows", "chan"),
        ),
        out_specs=(P(None, "rows", "chan"), P("rows", "chan")),
        check_vma=False,
    )
```

```python
import math

import jax
import jax.numpy as jnp
import numpy as np
from jax import lax
from jax.experimental import pallas as pl
from jax.experimental.pallas import tpu as pltpu
from jax.sharding import PartitionSpec as P

LS_STEPS = 4
time_step = 0.25
high = lax.Precision.HIGH


def np_angles(freqs, places, length):
    return 2.0 * math.pi / length * ((freqs[:, None] * places[None, :]) % length)


def with_halo(block, axis, dim, width):
    count = lax.axis_size(axis)
    forward = [(i, i + 1) for i in range(count - 1)]
    backward = [(target, source) for source, target in forward]
    size = block.shape[dim]
    low = lax.ppermute(lax.slice_in_dim(block, size - width, None, axis=dim), axis, forward)
    up = lax.ppermute(lax.slice_in_dim(block, 0, width, axis=dim), axis, backward)
    return jnp.concatenate([low, block, up], axis=dim)


def advance(phi, u, v, band):
    center = phi[1:-1, 1:-1]
    back_x = center - phi[:-2, 1:-1]
    ahead_x = phi[2:, 1:-1] - center
    back_y = center - phi[1:-1, :-2]
    ahead_y = phi[1:-1, 2:] - center
    transport = jnp.maximum(u, 0.0) * back_x + jnp.minimum(u, 0.0) * ahead_x
    transport = transport + jnp.maximum(v, 0.0) * back_y + jnp.minimum(v, 0.0) * ahead_y
    return center - time_step * band * transport


MESH = pl.DeviceIdType.MESH
f32 = jnp.float32
NT = (((1,), (1,)), ((), ()))
NN = (((1,), (0,)), ((), ()))
CW = 256


def split(x):
    hi = x.astype(jnp.bfloat16)
    return hi, (x - hi.astype(f32)).astype(jnp.bfloat16)


def np_split(x):
    x = x.astype(np.float32)
    hi = x.astype(jnp.bfloat16)
    lo = (x - hi.astype(np.float32)).astype(jnp.bfloat16)
    return jnp.asarray(hi), jnp.asarray(lo)


def dot3(a, b, dims):
    def one(x, y):
        return lax.dot_general(x, y, dims, preferred_element_type=f32)

    return one(a[0], b[0]) + (one(a[0], b[1]) + one(a[1], b[0]))


def spread(R, me, half, src, dst, send, recv):
    chan = lax.axis_index("chan")
    copies = []
    for step in range(1, R):
        to = lax.rem(me + step, R)
        copies.append(
            pltpu.make_async_remote_copy(
                src_ref=src.at[half, to],
                dst_ref=dst.at[half, me],
                send_sem=send.at[half * R + step],
                recv_sem=recv.at[half * R + step],
                device_id=(to, chan),
                device_id_type=MESH,
            )
        )
    return copies


def greet(R, me, chan):
    barrier = pltpu.get_barrier_semaphore()
    for step in range(1, R):
        pl.semaphore_signal(
            barrier, inc=1, device_id=(lax.rem(me + step, R), chan), device_id_type=MESH
        )
    pl.semaphore_signal(barrier, inc=1, device_id=(me, 1 - chan), device_id_type=MESH)
    return barrier


def forward_kernel(
    R, hid_in, fyh_in, fyl_in, txh_in, txl_in, out,
    hid, fyh, fyl, txh, txl, spec, got, xs, chs, chr_, ssem, rsem, csem, lsem,
):
    me = lax.axis_index("rows")
    chan = lax.axis_index("chan")
    cl, rc, ny = hid.shape
    ch = cl // 2
    pairs = [
        (fyh_in, fyh),
        (hid_in.at[pl.ds(0, ch)], hid.at[pl.ds(0, ch)]),
        (fyl_in, fyl),
        (hid_in.at[pl.ds(ch, ch)], hid.at[pl.ds(ch, ch)]),
        (txh_in, txh),
        (txl_in, txl),
    ]
    loads = [pltpu.make_async_copy(a, b, lsem.at[n]) for n, (a, b) in enumerate(pairs)]
    for load in loads:
        load.start()
    barrier = greet(R, me, chan)
    kc = 512
    half = cl * 8
    sent = []
    for h in range(2):
        for load in loads[0:3] if h == 0 else loads[3:4]:
            load.wait()
        acc = jnp.zeros((fyh.shape[0], ch * rc), f32)
        for j in range(ny // kc):
            cols = slice(j * kc, (j + 1) * kc)
            x = split(hid[h * ch : (h + 1) * ch, :, cols].reshape(ch * rc, kc))
            acc = acc + dot3((fyh[:, cols], fyl[:, cols]), x, NT)
        spec[h] = acc.reshape(spec.shape[1:])
        if h == 0:
            pl.semaphore_wait(barrier, R)
        copies = spread(R, me, h, spec, got, ssem, rsem)
        for copy in copies:
            copy.start()
        got[h, me] = spec[h, me]
        sent.append(copies)
    for h in range(2):
        for copy in sent[h]:
            copy.wait()
        for ri in range(2):
            for c in range(ch):
                at = ri * half + (h * ch + c) * 8
                xs[at : at + 8, :] = jnp.concatenate(
                    [got[h, s, ri * 8 : ri * 8 + 8, c * rc : (c + 1) * rc] for s in range(R)],
                    axis=1,
                )
    for load in loads[4:]:
        load.wait()
    g = dot3((txh[...], txl[...]), split(xs[...]), NT)
    mx = g.shape[0] // 2
    re = g[:mx, :half] + g[mx:, half:]
    im = g[:mx, half:] - g[mx:, :half]
    hp = mx // 2
    for d in range(2):
        chs[d, 0] = re[d * hp : (d + 1) * hp]
        chs[d, 1] = im[d * hp : (d + 1) * hp]
    copy = pltpu.make_async_remote_copy(
        src_ref=chs.at[1 - chan],
        dst_ref=chr_,
        send_sem=csem.at[0],
        recv_sem=csem.at[1],
        device_id=(me, 1 - chan),
        device_id_type=MESH,
    )
    copy.start()
    out[chan] = chs[chan]
    copy.wait()
    out[1 - chan] = chr_[...]


def inverse_kernel(
    R, hid_in, mixd, tih_in, til_in, iyh_in, iyl_in, gain, bias, pw, pb, mask_in, front, flags_in,
    vel, nxt,
    mall, chr_, isrc, igot, xs, xth, xtl, spc, psend, pgot, own, phi, ab,
    ssem, rsem, csem, psem, qsem, hs, hr,
    hid, tih, til, iyh, iyl, mask, flags, lsem,
):
    me = lax.axis_index("rows")
    chan = lax.axis_index("chan")
    cl, rc, ny = hid.shape
    half = cl * 8
    tw = ny // 2
    rh = rc // 2
    pairs = [
        (tih_in, tih), (til_in, til), (hid_in, hid), (iyh_in, iyh), (iyl_in, iyl),
        (mask_in, mask), (flags_in, flags),
    ]
    loads = [pltpu.make_async_copy(a, b, lsem.at[n]) for n, (a, b) in enumerate(pairs)]
    for load in loads:
        load.start()
    nch = tw // CW
    last = R - 1
    phi[...] = jnp.zeros_like(phi)
    ab[...] = jnp.zeros_like(ab)
    phi[8 : 8 + rc, 128 : 128 + tw] = front[...]
    barrier = greet(R, me, chan)

    for step in (1, R - 1):
        pl.semaphore_signal(
            barrier, inc=1, device_id=(lax.rem(me + step, R), 1 - chan), device_id_type=MESH
        )
    pl.semaphore_wait(barrier, R + 2)

    ccopy = pltpu.make_async_remote_copy(
        src_ref=mixd.at[1 - chan],
        dst_ref=chr_,
        send_sem=csem.at[0],
        recv_sem=csem.at[1],
        device_id=(me, 1 - chan),
        device_id_type=MESH,
    )
    ccopy.start()

    csrc = pl.multiple_of(tw - (tw - 128) * chan, 128)
    cdst = pl.multiple_of((tw + 128) * chan, 128)
    mid = (pl.ds(128, tw), pl.ds(128, tw))
    side = (pl.ds(csrc, 128), pl.ds(cdst, 128))
    up = (pl.ds(8, 8), pl.ds(8 + rc, 8))
    down = (pl.ds(rc, 8), pl.ds(0, 8))
    level = (pl.ds(8, rc), pl.ds(8, rc))
    moves = [(-1, 0, up, mid), (1, 0, down, mid), (0, 1, level, side), (-1, 1, up, side), (1, 1, down, side)]

    def halo(which, ref, act):
        for n, (dr, dc, rows, cols) in enumerate(moves):
            i = which * 5 + n
            lead = () if which == 0 else (slice(None),)
            copy = pltpu.make_async_remote_copy(
                src_ref=ref.at[lead + (rows[0], cols[0])],
                dst_ref=ref.at[lead + (rows[1], cols[1])],
                send_sem=hs.at[i],
                recv_sem=hr.at[i],
                device_id=(me + dr, 1 - chan if dc else chan),
                device_id_type=MESH,
            )
            first = (lambda: copy.start()) if act == "start" else (lambda: copy.wait_send())
            if dr == 0:
                first()
                if act == "wait":
                    copy.wait_recv()
            else:
                pl.when(me > 0 if dr < 0 else me < last)(first)
                if act == "wait":
                    pl.when(me < last if dr < 0 else me > 0)(lambda: copy.wait_recv())

    halo(0, phi, "start")

    mall[chan] = mixd[chan]
    ccopy.wait()
    mall[1 - chan] = chr_[...]
    re = jnp.concatenate([mall[0, 0], mall[1, 0]], axis=0)
    im = jnp.concatenate([mall[0, 1], mall[1, 1]], axis=0)
    full = jnp.concatenate(
        [jnp.concatenate([re, im], axis=1), jnp.concatenate([-im, re], axis=1)], axis=0
    )
    for load in loads[:2]:
        load.wait()
    res = dot3((tih[...], til[...]), split(full), NN)
    res = res.reshape(R, 2, rh, 2 * half)
    sent = []
    for h in range(2):
        isrc[h] = res[:, h]
        copies = spread(R, me, h, isrc, igot, ssem, rsem)
        for copy in copies:
            copy.start()
        igot[h, me] = isrc[h, me]
        sent.append(copies)

    def share(h, col):
        cols = pl.ds(pl.multiple_of(col, CW), CW)
        spc[...] = dot3((xth[...], xtl[...]), (iyh[:, cols], iyl[:, cols]), NN)
        u = jnp.zeros((rh, CW), f32)
        v = jnp.zeros((rh, CW), f32)
        for c in range(cl):
            skip = gain[c] * hid[c, h * rh : (h + 1) * rh, cols] + bias[c]
            z = spc[c * rh : (c + 1) * rh, :] + skip
            a = (0.5 * z) * (1.0 + lax.erf(z * (0.5**0.5)))
            u = u + pw[0, c] * a
            v = v + pw[1, c] * a
        return u, v

    def pcopy(h, j):
        return pltpu.make_async_remote_copy(
            src_ref=psend.at[h, j],
            dst_ref=pgot.at[h, j],
            send_sem=psem.at[h * nch + j],
            recv_sem=qsem.at[h * nch + j],
            device_id=(me, 1 - chan),
            device_id_type=MESH,
        )

    for h in range(2):
        for copy in sent[h]:
            copy.wait()
        for s in range(R):
            t = igot[h, s].T
            for ri in range(2):
                xs[s * 16 + ri * 8 : s * 16 + ri * 8 + 8, :] = jnp.concatenate(
                    [t[ri * half + c * 8 : ri * half + c * 8 + 8, :] for c in range(cl)], axis=1
                )
        xt = split(xs[...].T)
        xth[...] = xt[0]
        xtl[...] = xt[1]
        if h == 0:
            for load in loads[2:]:
                load.wait()

        def theirs(j, carry):
            u, v = share(h, (1 - chan) * tw + j * CW)
            psend[h, j, 0] = u
            psend[h, j, 1] = v
            pcopy(h, j).start()
            return carry

        def ours(j, carry):
            u, v = share(h, chan * tw + j * CW)
            own[h, j, 0] = u
            own[h, j, 1] = v
            return carry

        lax.fori_loop(0, nch, theirs, 0)
        lax.fori_loop(0, nch, ours, 0)
    for h in range(2):
        rows = slice(h * rh, (h + 1) * rh)
        for j in range(nch):
            pcopy(h, j).wait()
            cols = slice(j * CW, (j + 1) * CW)
            ice = mask[rows, cols].astype(f32)
            band = flags[rows, cols].astype(f32) * time_step
            for k in range(2):
                w = (own[h, j, k] + pgot[h, j, k] + pb[k]) * ice
                vel[k, rows, cols] = w
                ab[k, 8 + h * rh : 8 + (h + 1) * rh, 128 + j * CW : 128 + (j + 1) * CW] = w * band
    halo(1, ab, "start")
    halo(0, phi, "wait")
    halo(1, ab, "wait")
    a = ab[0]
    b = ab[1]
    ap, am = jnp.maximum(a, 0.0), jnp.minimum(a, 0.0)
    bp, bm = jnp.maximum(b, 0.0), jnp.minimum(b, 0.0)
    x = phi[...]
    nr, nc = x.shape
    for _ in range(LS_STEPS):
        move = ap * (x - pltpu.roll(x, 1, 0)) + am * (pltpu.roll(x, nr - 1, 0) - x)
        move = move + (bp * (x - pltpu.roll(x, 1, 1)) + bm * (pltpu.roll(x, nc - 1, 1) - x))
        x = x - move
    nxt[...] = x[8 : 8 + rc, 128 : 128 + tw]


def on_kernels(
    hidden, front, spectral_weight, skip_gain, skip_bias, project_weight, project_bias,
    ice_mask, front_flags,
):
    cl, rc, ny = hidden.shape
    R = lax.axis_size("rows")
    D = lax.axis_size("chan")
    ql = spectral_weight.shape[1]
    pn = spectral_weight.shape[2]
    nx, mx, my = rc * R, pn * D, ql * R
    scale = 1.0 / math.sqrt(nx * ny * mx * my)
    yph = np_angles(np.arange(my), np.arange(ny), ny).reshape(R, ql, ny)
    fy = np.stack([np.cos(yph), -np.sin(yph)], axis=1).reshape(2 * my, ny)
    w = np.where(np.arange(my) == 0, 1.0, 2.0).reshape(R, ql, 1) * scale
    iy = np.stack([w * np.cos(yph), -w * np.sin(yph)], axis=1).reshape(2 * my, ny)
    pid = np.arange(mx)
    xph = np_angles(np.where(pid < mx // 2, pid, pid - mx), np.arange(nx), nx)
    tx = np.concatenate([np.cos(xph), np.sin(xph)], axis=0)
    vm = pl.BlockSpec(memory_space=pltpu.VMEM)
    sm = pl.BlockSpec(memory_space=pltpu.SMEM)
    hbm = pl.BlockSpec(memory_space=pltpu.HBM)
    bf16 = jnp.bfloat16
    dma = pltpu.SemaphoreType.DMA
    lanes = cl * ql

    def kernel_a(*refs):
        forward_kernel(R, *refs)

    def kernel_b(*refs):
        inverse_kernel(R, *refs)

    spec = pl.pallas_call(
        kernel_a,
        out_shape=jax.ShapeDtypeStruct((D, 2, pn, lanes), f32),
        in_specs=[hbm] * 5,
        out_specs=vm,
        scratch_shapes=[
            pltpu.VMEM((cl, rc, ny), f32),
            pltpu.VMEM((2 * my, ny), bf16),
            pltpu.VMEM((2 * my, ny), bf16),
            pltpu.VMEM((2 * mx, nx), bf16),
            pltpu.VMEM((2 * mx, nx), bf16),
            pltpu.VMEM((2, R, 2 * ql, cl // 2 * rc), f32),
            pltpu.VMEM((2, R, 2 * ql, cl // 2 * rc), f32),
            pltpu.VMEM((2 * lanes, nx), f32),
            pltpu.VMEM((D, 2, pn, lanes), f32),
            pltpu.VMEM((2, pn, lanes), f32),
            dma((2 * R,)),
            dma((2 * R,)),
            dma((2,)),
            dma((6,)),
        ],
        compiler_params=pltpu.CompilerParams(
            collective_id=0, has_side_effects=True, vmem_limit_bytes=60 * 2**20
        ),
        name="forward",
    )(hidden, *np_split(fy), *np_split(tx))
    spec = spec.reshape(D, 2, pn, cl, ql).transpose(1, 0, 3, 4, 2).reshape(2, D * cl, ql, pn)
    wt = spectral_weight.transpose(0, 3, 4, 1, 2)
    a, b = spec[0][:, None], spec[1][:, None]
    re = jnp.sum(wt[0] * a - wt[1] * b, axis=0)
    im = jnp.sum(wt[0] * b + wt[1] * a, axis=0)
    mixed = jnp.stack([re, im]).reshape(2, D, cl, ql, pn).transpose(1, 0, 4, 2, 3)
    mixed = mixed.reshape(D, 2, pn, lanes)
    nch = ny // D // CW
    tw = ny // D
    return pl.pallas_call(
        kernel_b,
        out_shape=(
            jax.ShapeDtypeStruct((2, rc, tw), f32),
            jax.ShapeDtypeStruct((rc, tw), f32),
        ),
        in_specs=[hbm, vm] + [hbm] * 4 + [sm] * 4 + [hbm, vm, hbm],
        out_specs=(vm, vm),
        scratch_shapes=[
            pltpu.VMEM((D, 2, pn, lanes), f32),
            pltpu.VMEM((2, pn, lanes), f32),
            pltpu.VMEM((2, R, rc // 2, 2 * lanes), f32),
            pltpu.VMEM((2, R, rc // 2, 2 * lanes), f32),
            pltpu.VMEM((2 * my, cl * rc // 2), f32),
            pltpu.VMEM((cl * rc // 2, 2 * my), bf16),
            pltpu.VMEM((cl * rc // 2, 2 * my), bf16),
            pltpu.VMEM((cl * rc // 2, CW), f32),
            pltpu.VMEM((2, nch, 2, rc // 2, CW), f32),
            pltpu.VMEM((2, nch, 2, rc // 2, CW), f32),
            pltpu.VMEM((2, nch, 2, rc // 2, CW), f32),
            pltpu.VMEM((rc + 16, tw + 256), f32),
            pltpu.VMEM((2, rc + 16, tw + 256), f32),
            dma((2 * R,)),
            dma((2 * R,)),
            dma((2,)),
            dma((2 * nch,)),
            dma((2 * nch,)),
            dma((10,)),
            dma((10,)),
            pltpu.VMEM((cl, rc, ny), f32),
            pltpu.VMEM((nx, 2 * mx), bf16),
            pltpu.VMEM((nx, 2 * mx), bf16),
            pltpu.VMEM((2 * my, ny), bf16),
            pltpu.VMEM((2 * my, ny), bf16),
            pltpu.VMEM((rc, tw), jnp.int32),
            pltpu.VMEM((rc, tw), jnp.int32),
            dma((7,)),
        ],
        compiler_params=pltpu.CompilerParams(
            collective_id=1, has_side_effects=True, vmem_limit_bytes=57 * 2**20
        ),
        name="inverse",
    )(
        hidden, mixed, *np_split(tx.T), *np_split(iy), skip_gain, skip_bias,
        project_weight, project_bias, ice_mask, front, front_flags,
    )


def on_device(
    hidden,
    front,
    spectral_weight,
    skip_gain,
    skip_bias,
    project_weight,
    project_bias,
    ice_mask,
    front_flags,
):
    cl, rc, ny = hidden.shape
    R = lax.axis_size("rows")
    D = lax.axis_size("chan")
    ql = spectral_weight.shape[1]
    if D == 2 and ql == 8 and cl * ql == 128 and rc % 16 == 0 and (rc * R) % 128 == 0:
        return on_kernels(
            hidden, front, spectral_weight, skip_gain, skip_bias, project_weight,
            project_bias, ice_mask, front_flags,
        )
    pl_ = spectral_weight.shape[2]
    nx = rc * R
    mx = pl_ * D
    my = ql * R
    scale = 1.0 / math.sqrt(nx * ny * mx * my)
    yph = np_angles(np.arange(my), np.arange(ny), ny)
    fy = np.stack([np.cos(yph), -np.sin(yph)], axis=1).reshape(2 * my, ny).astype(np.float32)
    w = np.where(np.arange(my) == 0, 1.0, 2.0)[:, None] * scale
    iy = np.stack([w * np.cos(yph), -w * np.sin(yph)], axis=1).reshape(2 * my, ny).astype(np.float32)
    pid = np.arange(mx)
    kp = np.where(pid < mx // 2, pid, pid - mx)
    xph = np_angles(kp, np.arange(nx), nx)
    cx = np.cos(xph).astype(np.float32)
    sx = np.sin(xph).astype(np.float32)
    fx = np.stack([np.stack([cx, -sx]), np.stack([sx, cx])]).transpose(0, 3, 1, 2).reshape(2, nx, 2 * mx)
    ix = np.stack([np.stack([cx, sx]), np.stack([-sx, cx])]).reshape(2, 2, mx, nx)

    spec_y = jnp.einsum("ky,cxy->kcx", jnp.asarray(fy), hidden, precision=high)
    recv = lax.all_to_all(spec_y.reshape(R, ql, 2, cl, rc), "rows", 0, 0, tiled=True)
    spec = jnp.einsum(
        "sqrcx,rsxP->qcP", recv, jnp.asarray(fx).reshape(2, R, rc, 2 * mx), precision=high
    ).reshape(ql, cl, 2, D, pl_)
    spec = lax.all_to_all(spec.transpose(3, 1, 2, 0, 4), "chan", 0, 0, tiled=True)
    spec = spec.reshape(D * cl, 2, ql, pl_)
    wt = spectral_weight.transpose(0, 3, 4, 1, 2)
    a, b = spec[:, 0][:, None], spec[:, 1][:, None]
    re = jnp.sum(wt[0] * a - wt[1] * b, axis=0)
    im = jnp.sum(wt[0] * b + wt[1] * a, axis=0)
    mixed = jnp.stack([re, im], axis=1).reshape(D, cl, 2, ql, pl_)
    mixed = lax.all_to_all(mixed, "chan", 0, 0, tiled=True)
    inv = jnp.einsum(
        "dcrqp,rtdpx->xqtc", mixed, jnp.asarray(ix).reshape(2, 2, D, pl_, nx), precision=high
    ).transpose(1, 2, 3, 0).reshape(ql, 2, cl, R, rc)
    inv = lax.all_to_all(inv.transpose(3, 0, 1, 2, 4), "rows", 0, 0, tiled=True)
    inv = inv.reshape(2 * my, cl, rc)
    spectral = jnp.einsum("kcx,ky->cxy", inv, jnp.asarray(iy), precision=high)
    act = jax.nn.gelu(
        spectral + skip_gain[:, None, None] * hidden + skip_bias[:, None, None], approximate=False
    )
    part = jnp.stack(
        [jnp.sum(project_weight[j][:, None, None] * act, axis=0) for j in range(2)]
    )
    part = part.reshape(2, rc, D, ny // D).transpose(2, 0, 1, 3)
    got = lax.all_to_all(part, "chan", 0, 0, tiled=True)
    speed = jnp.sum(got, axis=0) + project_bias[:, None, None]
    velocity = speed * ice_mask.astype(jnp.float32)[None]
    band = front_flags.astype(jnp.float32)
    W = LS_STEPS
    state = jnp.concatenate([velocity, band[None], front[None]], axis=0)
    state = with_halo(with_halo(state, "rows", 1, W), "chan", 2, W)
    u, v, bd, level = state[0], state[1], state[2], state[3]
    for step in range(LS_STEPS):
        i = step + 1
        level = advance(level, u[i:-i, i:-i], v[i:-i, i:-i], bd[i:-i, i:-i])
    return (velocity, level)


def solution(mesh):
    return jax.shard_map(
        on_device,
        mesh=mesh,
        in_specs=(
            P("chan", "rows", None),
            P("rows", "chan"),
            P(None, "rows", "chan", None, None),
            P("chan"),
            P("chan"),
            P(None, "chan"),
            P(),
            P("rows", "chan"),
            P("rows", "chan"),
        ),
        out_specs=(P(None, "rows", "chan"), P("rows", "chan")),
        check_vma=False,
    )
```
